32 devices in a mesh: branch: 2 (over y), ctx: 8 (over z, x), tp: 2 (over core).
Axes of the slice: x: 2, y: 2, z: 4, core: 2. Of those that a mesh axis runs over, the one named last changes fastest.
Arguments:
- queries: bfloat16 [2, 2048, 8192], P('branch', 'ctx', 'tp'), may hold values from -12 to 12
- keys: bfloat16 [2, 2048, 1024], P('branch', 'ctx', 'tp'), may hold values from -12 to 12
- values: bfloat16 [2, 2048, 1024], P('branch', 'ctx', 'tp'), may hold values from -800 to 800
- segments: int32 [2048], replicated, may hold values from 0 to 3, never falling along the last dimension, each value on 1 to 1024 neighbouring positions
- norm_gain: float32 [2, 8192], P('branch', 'tp'), may hold values from 0.5 to 1.5
- head_weight: float32 [2, 8192], P('branch', 'tp'), may hold values from -0.0625 to 0.0625
Outputs:
- normed: bfloat16 [2, 2048, 8192], P('branch', 'ctx', 'tp')
- joined: float32 [2048], P('ctx')
The draws below stay inside these ranges and needn't reach their ends.
Inputs may be any that keep to these rules, and one draw needn't show every extreme that they name: `segments`: rollout ids never fall along the sequence; each rollout holds 1 to 1024 tokens, and one holds exactly 1024.
All inputs are finite; a program needn't handle non-finite values.
Results may differ from the reference program's by a relative error of at most 0.007.
Values may be sent and summed in bfloat16 or wider, within the bound.
A program may use at most 64 MiB of HBM per device.

```python
import math
import jax
import jax.numpy as jnp
import numpy as np
from jax import lax

H = 64
KVH = 8
HD = 128
COUNT = 4
D = 8192
L = 2048
MOST = 1024


def draw_queries(key, part):
    noise_key = jax.random.fold_in(key, 11)
    drawn = jnp.clip(jax.random.normal(noise_key, (2, L, D), jnp.float32), -4.0, 4.0)
    return drawn.astype(jnp.bfloat16)


def draw_keys(key, part):
    noise_key = jax.random.fold_in(key, 17)
    drawn = jnp.clip(jax.random.normal(noise_key, (2, L, KVH * HD), jnp.float32), -4.0, 4.0)
    return drawn.astype(jnp.bfloat16)


def draw_values(key, part):
    noise_key, column_key, row_key = jax.random.split(jax.random.fold_in(key, 31), 3)
    columns = KVH * HD
    head_number = (jnp.arange(columns) // HD).astype(jnp.float32)
    drawn = jnp.clip(jax.random.normal(noise_key, (2, L, columns), jnp.float32), -4.0, 4.0)
    rising = 1.0 + head_number / max(KVH - 1, 1)
    column_scale = jnp.exp(jax.random.uniform(column_key, (2, 1, columns), jnp.float32) * math.log(10.0))
    row_scale = jnp.exp(jax.random.uniform(row_key, (2, L, 1), jnp.float32) * math.log(10.0))
    return (drawn * rising * column_scale * row_scale).astype(jnp.bfloat16)


def block_scale(own_key, extent, cuts, low, largest):
    def one(axis_at, parts):
        heights = jax.random.uniform(jax.random.fold_in(jax.random.fold_in(own_key, 6), axis_at), (parts,), jnp.float32, low / len(cuts), largest / len(cuts))
        return jnp.repeat(jnp.exp(heights), extent[axis_at] // parts).reshape((-1,) + (1,) * (len(extent) - axis_at - 1))

    loudness = one(*cuts[0])
    for cut in cuts[1:]:
        loudness = loudness * one(*cut)
    return loudness


def profile(count, total, limit, lean):
    portions = [(1 << 20) // math.isqrt(grade ** lean) + 1 for grade in range(2, count + 1)]
    rest, holding = total - limit - (count - 1), [1] * (count - 1)
    while rest > 0:
        candidates = [i for i in range(count - 1) if holding[i] < limit]
        whole, left = sum([portions[i] for i in candidates]), rest
        for i in candidates:
            extra = min(limit - holding[i], max(1, left * portions[i] // whole), rest)
            holding[i] = holding[i] + extra
            rest = rest - extra
    return np.array([limit] + holding)


def uneven_parts(own_key, count, total, reach, slope):
    if count == 2:
        one = jax.random.randint(own_key, (), max(1, total - reach), min(reach, total - 1) + 1)
        return jnp.stack([one, total - one])
    tallies = jnp.asarray(profile(count, total, reach, slope), jnp.int32)
    twos = (count - 1) // 2
    giver, sink = tallies[1:1 + 2 * twos:2], tallies[2:2 + 2 * twos:2]
    room = jnp.minimum(giver - 1, reach - sink)
    passed = jax.random.randint(jax.random.fold_in(own_key, 1), (twos,), 0, 1 << 20) % (room + 1)
    tallies = tallies.at[1:1 + 2 * twos:2].set(giver - passed).at[2:2 + 2 * twos:2].set(sink + passed)
    return tallies[jax.random.permutation(jax.random.fold_in(own_key, 2), count)]


def scatter_about(key, shape, scale, bound, shards=(), kind=jnp.bfloat16):
    level = block_scale(key, shape, shards, -0.22, 0.18) if shards else 1.0
    values = jax.random.normal(key, shape, jnp.float32) * scale * level
    return jnp.minimum(jnp.maximum(values, -bound), bound).astype(kind)


def setup_inputs(seed: int = 0) -> dict:
    key_of = jax.random.split(jax.random.key(seed), 7)
    return {
        "queries": draw_queries(jax.random.fold_in(key_of[6], 71), 0),
        "keys": draw_keys(jax.random.fold_in(key_of[6], 71), 0),
        "values": draw_values(jax.random.fold_in(key_of[6], 71), 0),
        "segments": jnp.searchsorted(jnp.cumsum(uneven_parts(key_of[3], COUNT, L, MOST, 1)), jnp.arange(L), side="right").astype(jnp.int32),
        "norm_gain": jnp.clip(1.0 + 0.1 * jax.random.normal(key_of[4], (2, D), jnp.float32), 0.5, 1.5),
        "head_weight": scatter_about(key_of[5], (2, D), D ** -0.5, 0.0625, ((0, 2), (1, 2)), jnp.float32),
    }


NEGATIVE = -1e+30
EPSILON = 1e-06

def attend(queries, keys, values, segments):
    per_group = H // KVH
    block_rows = min(L, 256)
    query_heads = queries.astype(jnp.float32).reshape(L, KVH, per_group, HD)
    key_heads = keys.astype(jnp.float32).reshape(L, KVH, HD)
    value_heads = values.astype(jnp.float32).reshape(L, KVH, HD)
    positions = jnp.arange(L, dtype=jnp.int32)

    def visit_block(number):
        begin = (number * block_rows).astype(jnp.int32)
        query_block = lax.dynamic_slice_in_dim(query_heads, begin, block_rows, 0)
        query_pos = begin + jnp.arange(block_rows, dtype=jnp.int32)
        query_seg = lax.dynamic_slice_in_dim(segments, begin, block_rows, 0)
        scores = jnp.einsum('tkgd,pkd->kgtp', query_block, key_heads) * (1.0 / math.sqrt(HD))
        allowed = (segments[None, :] == query_seg[:, None]) & (positions[None, :] <= query_pos[:, None])
        scores = jnp.where(allowed, scores, NEGATIVE)
        maxima = lax.optimization_barrier(jnp.max(scores, axis=-1, keepdims=True))
        weights = jnp.where(allowed, jnp.exp(scores - maxima), 0.0)
        totals = lax.optimization_barrier(jnp.sum(weights, axis=-1))
        rounded = lax.optimization_barrier(weights.astype(jnp.bfloat16)).astype(jnp.float32)
        mixed = jnp.einsum('kgtp,pkd->tkgd', rounded, value_heads)
        mixed = mixed / jnp.transpose(totals, (2, 0, 1))[..., None]
        return mixed.reshape(block_rows, D).astype(jnp.bfloat16)
    blocks = lax.map(visit_block, jnp.arange(L // block_rows, dtype=jnp.int32))
    return blocks.reshape(L, D)

def reference(queries, keys, values, segments, norm_gain, head_weight):
    normed_list = []
    score_list = []
    for section in range(2):
        attn_rows = attend(queries[section], keys[section], values[section], segments)
        attended = lax.optimization_barrier(attn_rows).astype(jnp.float32)
        inverse = lax.rsqrt(lax.optimization_barrier(jnp.mean(attended * attended, axis=-1)) + EPSILON)
        scaled = attended * inverse[:, None] * norm_gain[section].astype(jnp.float32)
        normed_list.append(scaled.astype(jnp.bfloat16))
        score_list.append(lax.optimization_barrier(jnp.sum(scaled * head_weight[section].astype(jnp.float32), axis=-1)))
    return (jnp.stack(normed_list), score_list[0] + score_list[1])
```

```python
import functools
import math

import jax
import jax.numpy as jnp
from jax import lax
from jax.experimental import pallas as pl
from jax.experimental.pallas import tpu as pltpu
from jax.sharding import PartitionSpec as P

H = 64
KVH = 8
HD = 128
D = 8192

BIG = 2.0**100
EPSILON = 1e-06
MESH = pl.DeviceIdType.MESH


def kernel(
    sizes, q_hbm, k_hbm, v_hbm, seg_ref, gain_ref, weight_ref,
    att_ref, inv_ref, joined_ref,
    q_vm, kv, gmask, fmask, acc, best, squares, scored, stats,
    q_sem, own_sem, col_send, col_recv, x_send, x_recv, st_send, st_recv,
):
    n, branches, tps, span = sizes
    steps = span // 2
    rows = q_vm.shape[0]
    half = rows // 2
    groups = kv.shape[0]
    per_group = H // KVH
    window = kv.shape[2]
    scale = math.log2(math.e) / math.sqrt(HD)
    me = lax.axis_index("ctx")
    b_me, t_me = lax.axis_index("branch"), lax.axis_index("tp")
    side = lax.rem(me, 2)
    partner = me + 1 - 2 * side
    has_next = me + 2 < n
    mine = b_me * tps + t_me

    q_copy = pltpu.make_async_copy(q_hbm.at[0], q_vm, q_sem)
    own = []
    for g in range(groups):
        for part, source in enumerate((k_hbm, v_hbm)):
            own.append(
                pltpu.make_async_copy(
                    source.at[0, :, pl.ds(g * HD, HD)],
                    kv.at[g, part, pl.ds(span * rows, rows), :],
                    own_sem.at[g, part],
                )
            )
    for copy in own:
        copy.start()
    q_copy.start()

    peers = []
    for db in range(branches):
        for dt in range(tps):
            if db or dt:
                peers.append((lax.rem(b_me + db, branches), lax.rem(t_me + dt, tps)))

    barrier = pltpu.get_barrier_semaphore()

    @pl.when(me >= 2)
    def _():
        pl.semaphore_signal(barrier, inc=1, device_id={"ctx": me - 2}, device_id_type=MESH)

    @pl.when(has_next)
    def _():
        pl.semaphore_signal(barrier, inc=1, device_id={"ctx": me + 2}, device_id_type=MESH)

    pl.semaphore_signal(barrier, inc=1, device_id={"ctx": partner}, device_id_type=MESH)
    for b_to, t_to in peers:
        pl.semaphore_signal(
            barrier, inc=1, device_id={"branch": b_to, "tp": t_to}, device_id_type=MESH
        )

    lane = lax.broadcasted_iota(jnp.int32, (1, HD), 1)
    segs = seg_ref[...]
    total = segs.shape[0] * segs.shape[1]
    far = 2.0**30
    low = jnp.where(lane == 0, 0.0, jnp.where(lane == 4, -far, far))
    high = jnp.where(lane == 3, float(total), jnp.where(lane == 4, 0.0, -far))
    for rollout in range(1, 4):
        count = jnp.sum((segs < rollout).astype(jnp.float32), axis=1, keepdims=True)
        count = jnp.sum(count, axis=0, keepdims=True)
        low = jnp.where(lane == rollout, count, low)
        high = jnp.where(lane == rollout - 1, count, high)
    place = lax.broadcasted_iota(jnp.int32, (window, HD), 0) + (me - span) * rows
    place = place.astype(jnp.float32)
    member = jnp.where((place >= low) & (place < high), 1.0, 0.0)
    gmask[...] = member.astype(jnp.bfloat16)
    fmask[...] = ((member[span * rows :] - 1.0) * BIG).astype(jnp.bfloat16)
    squares[...] = jnp.zeros_like(squares)
    scored[...] = jnp.zeros_like(scored)

    for distance in range(1, span + 1):

        @pl.when(me < distance)
        def _(distance=distance):
            kv[:, :, pl.ds((span - distance) * rows, rows), :] = jnp.zeros(
                (groups, 2, rows, HD), jnp.bfloat16
            )

    def col_copy(step, g):
        return pltpu.make_async_remote_copy(
            src_ref=kv.at[g, :, pl.ds((span - 2 * (step - 1)) * rows, rows), :],
            dst_ref=kv.at[g, :, pl.ds((span - 2 * step) * rows, rows), :],
            send_sem=col_send.at[step - 1, g],
            recv_sem=col_recv.at[step - 1, g],
            device_id={"ctx": me + 2},
            device_id_type=MESH,
        )

    def x_copy(u, g):
        first = pl.multiple_of((span - 2 * u - 2 * side) * rows, rows)
        return pltpu.make_async_remote_copy(
            src_ref=kv.at[g, :, pl.ds(first, rows), :],
            dst_ref=kv.at[g, :, pl.ds((span - 2 * u - 1) * rows, rows), :],
            send_sem=x_send.at[u, g],
            recv_sem=x_recv.at[u, g],
            device_id={"ctx": partner},
            device_id_type=MESH,
        )

    pl.semaphore_wait(
        barrier,
        1 + len(peers) + (me >= 2).astype(jnp.int32) + has_next.astype(jnp.int32),
    )

    for g in range(groups):
        own[2 * g].wait()
        own[2 * g + 1].wait()

        @pl.when(has_next)
        def _(g=g):
            col_copy(1, g).start()

        @pl.when(side == 0)
        def _(g=g):
            x_copy(0, g).start()

    def arrive(step, g):
        @pl.when(me >= 2 * step)
        def _():
            col_copy(step, g).wait_recv()
            if step < steps:

                @pl.when(has_next)
                def _():
                    col_copy(step + 1, g).start()

                @pl.when(side == 0)
                def _():
                    x_copy(step, g).start()

            @pl.when(side == 1)
            def _():
                x_copy(step - 1, g).start()

    tri_row = lax.broadcasted_iota(jnp.int32, (2 * half, half), 0)
    tri_col = lax.broadcasted_iota(jnp.int32, (2 * half, half), 1)
    causal = tri_col <= lax.rem(tri_row, half)

    def pair(step, g, index):
        top = g * per_group + 2 * index
        for r in range(2):
            lines = pl.ds(r * half, half)
            first, last = (span - 2 * step) * rows, (span - 2 * step + 2) * rows
            if step == 1:
                last = span * rows + (r + 1) * half
            if step == steps:
                first += r * half
            keys = pl.ds(first, last - first)
            columns = [pl.ds(pl.multiple_of((top + e) * HD, HD), HD) for e in range(2)]
            marks = fmask[lines, :]
            left = jnp.concatenate(
                [
                    jnp.concatenate([q_vm[lines, columns[0]], q_vm[lines, columns[1]]], axis=0),
                    jnp.concatenate([marks, marks], axis=0),
                ],
                axis=1,
            )
            right = jnp.concatenate([kv[g, 0, keys, :], gmask[keys, :]], axis=1)
            scores = lax.dot_general(
                left, right, (((1,), (1,)), ((), ())), preferred_element_type=jnp.float32
            )
            if step == 1:
                body = last - first - half
                scores = jnp.concatenate(
                    [scores[:, :body], jnp.where(causal, scores[:, body:], -BIG)], axis=1
                )
            peak = jnp.max(scores, axis=1, keepdims=True)
            if step > 1:
                before = best[top, lines, :], best[top + 1, lines, :]
                before = jnp.concatenate(before, axis=0)
                wide = jnp.maximum(before, peak)
                peak = wide[:, :1]
            weights = jnp.exp2((scores - peak) * scale).astype(jnp.bfloat16)
            mixer = jnp.concatenate(
                [kv[g, 1, keys, :], jnp.ones((last - first, HD), jnp.bfloat16)], axis=1
            )
            mixed = jnp.dot(weights, mixer, preferred_element_type=jnp.float32)
            if step > 1:
                shrink = jnp.exp2((before - wide) * scale)
                earlier = jnp.concatenate(
                    [acc[top, lines, :], acc[top + 1, lines, :]], axis=0
                )
                mixed = mixed + earlier * jnp.concatenate([shrink, shrink], axis=1)
            if step < steps:
                acc[top, lines, :] = mixed[:half]
                acc[top + 1, lines, :] = mixed[half:]
                wide = jnp.broadcast_to(peak, (2 * half, HD))
                best[top, lines, :] = wide[:half]
                best[top + 1, lines, :] = wide[half:]
            else:
                attended = (mixed[:, :HD] / mixed[:, HD:]).astype(jnp.bfloat16)
                for e in range(2):
                    out = attended[e * half : (e + 1) * half]
                    att_ref[lines, columns[e]] = out
                    out = out.astype(jnp.float32)
                    line = gain_ref[:, columns[e]] * weight_ref[:, columns[e]]
                    squares[lines, :] += out * out
                    scored[lines, :] += out * line

    units = [(step, g) for step in range(1, steps + 1) for g in range(groups)]
    pairs = per_group // 2
    arrive(*units[0])
    q_copy.wait()
    for number, (step, g) in enumerate(units):

        @pl.when(me >= 2 * step - 1)
        def _(step=step, g=g):
            x_copy(step - 1, g).wait_recv()

        def walk(index, carry, step=step, g=g):
            pair(step, g, index)
            return carry

        lax.fori_loop(0, pairs // 2, walk, 0)
        if number + 1 < len(units):
            arrive(*units[number + 1])
        lax.fori_loop(pairs // 2, pairs, walk, 0)

    slab = jnp.concatenate(
        [
            jnp.sum(squares[...].T, axis=0, keepdims=True),
            jnp.sum(scored[...].T, axis=0, keepdims=True),
            jnp.zeros((6, rows), jnp.float32),
        ],
        axis=0,
    )
    stats[mine] = slab

    def stat_copy(number):
        b_to, t_to = peers[number]
        return pltpu.make_async_remote_copy(
            src_ref=stats.at[mine],
            dst_ref=stats.at[mine],
            send_sem=st_send.at[number],
            recv_sem=st_recv.at[number],
            device_id={"branch": b_to, "tp": t_to},
            device_id_type=MESH,
        )

    for number in range(len(peers)):
        stat_copy(number).start()

    for g in range(groups):
        for step in range(1, steps + 1):

            @pl.when(has_next & (me >= 2 * (step - 1)))
            def _(step=step, g=g):
                col_copy(step, g).wait_send()

            @pl.when(me >= 2 * (step - 1 + side))
            def _(step=step, g=g):
                x_copy(step - 1, g).wait_send()

    for number in range(len(peers)):
        stat_copy(number).wait()

    def inverse_of(branch):
        square_sum = stats[branch * tps, 0:1, :]
        score = stats[branch * tps, 1:2, :]
        for t in range(1, tps):
            square_sum = square_sum + stats[branch * tps + t, 0:1, :]
            score = score + stats[branch * tps + t, 1:2, :]
        return lax.rsqrt(square_sum / D + EPSILON), score

    joined = jnp.zeros((1, rows), jnp.float32)
    for branch in range(branches):
        inverse, score = inverse_of(branch)
        joined = joined + inverse * score
    joined_ref[...] = joined
    inverse, _ = inverse_of(b_me)
    inv_ref[...] = jnp.broadcast_to(inverse, (HD, rows)).T


def local(sizes, queries, keys, values, segments, norm_gain, head_weight):
    n, branches, tps, span = sizes
    rows, columns = queries.shape[1:]
    groups = keys.shape[2] // HD
    heads = columns // HD
    window = (span + 1) * rows
    steps = span // 2
    devices = branches * tps
    vmem = pl.BlockSpec(memory_space=pltpu.VMEM)
    hbm = pl.BlockSpec(memory_space=pl.ANY)
    dma = pltpu.SemaphoreType.DMA
    attended, inverse, joined = pl.pallas_call(
        functools.partial(kernel, sizes),
        out_shape=(
            jax.ShapeDtypeStruct((rows, columns), jnp.bfloat16),
            jax.ShapeDtypeStruct((rows, HD), jnp.float32),
            jax.ShapeDtypeStruct((1, rows), jnp.float32),
        ),
        in_specs=[hbm, hbm, hbm, vmem, vmem, vmem],
        out_specs=(vmem, vmem, vmem),
        scratch_shapes=[
            pltpu.VMEM((rows, columns), jnp.bfloat16),
            pltpu.VMEM((groups, 2, window, HD), jnp.bfloat16),
            pltpu.VMEM((window, HD), jnp.bfloat16),
            pltpu.VMEM((rows, HD), jnp.bfloat16),
            pltpu.VMEM((heads, rows, 2 * HD), jnp.float32),
            pltpu.VMEM((heads, rows, HD), jnp.float32),
            pltpu.VMEM((rows, HD), jnp.float32),
            pltpu.VMEM((rows, HD), jnp.float32),
            pltpu.VMEM((devices, 8, rows), jnp.float32),
            dma,
            dma((groups, 2)),
            dma((steps, groups)),
            dma((steps, groups)),
            dma((steps, groups)),
            dma((steps, groups)),
            dma((devices - 1,)),
            dma((devices - 1,)),
        ],
        compiler_params=pltpu.CompilerParams(
            collective_id=0, has_side_effects=True, vmem_limit_bytes=48 * 2**20
        ),
        cost_estimate=pl.CostEstimate(
            flops=4 * rows * window * columns,
            bytes_accessed=4 * rows * columns,
            transcendentals=heads * rows * window,
        ),
    )(queries, keys, values, segments.reshape(-1, HD), norm_gain, head_weight)
    normed = attended.astype(jnp.float32) * inverse[:, :1] * norm_gain
    return normed.astype(jnp.bfloat16)[None], joined.reshape(rows)


def solution(mesh):
    n = mesh.shape["ctx"]
    sizes = (n, mesh.shape["branch"], mesh.shape["tp"], n // 2)
    return jax.shard_map(
        functools.partial(local, sizes),
        mesh=mesh,
        in_specs=(
            P("branch", "ctx", "tp"),
            P("branch", "ctx", "tp"),
            P("branch", "ctx", "tp"),
            P(),
            P("branch", "tp"),
            P("branch", "tp"),
        ),
        out_specs=(P("branch", "ctx", "tp"), P("ctx")),
        check_vma=False,
    )
```

```python
import functools
import math

import jax
import jax.numpy as jnp
from jax import lax
from jax.experimental import pallas as pl
from jax.experimental.pallas import tpu as pltpu
from jax.sharding import PartitionSpec as P

H = 64
KVH = 8
HD = 128
D = 8192

BIG = 2.0**100
EPSILON = 1e-06
MESH = pl.DeviceIdType.MESH


def kernel(
    sizes, q_hbm, k_hbm, v_hbm, seg_hbm, gain_hbm, weight_hbm,
    att_ref, inv_ref, joined_ref,
    q_vm, kv, vt, gmask, fmask, acc, best, squares, scored, stats, seg_ref, gain_ref, weight_ref,
    q_sem, own_sem, row_sem, col_send, col_recv, x_send, x_recv, st_send, st_recv,
):
    n, branches, tps, span = sizes
    steps = span // 2
    rows = q_vm.shape[0]
    half = rows // 2
    groups = kv.shape[0]
    per_group = H // KVH
    window = kv.shape[2]
    scale = math.log2(math.e) / math.sqrt(HD)
    me = lax.axis_index("ctx")
    b_me, t_me = lax.axis_index("branch"), lax.axis_index("tp")
    side = lax.rem(me, 2)
    partner = me + 1 - 2 * side
    has_next = me + 2 < n
    mine = b_me * tps + t_me

    q_copy = pltpu.make_async_copy(q_hbm.at[0], q_vm, q_sem)
    own = []
    for g in range(groups):
        for part, source in enumerate((k_hbm, v_hbm)):
            own.append(
                pltpu.make_async_copy(
                    source.at[0, :, pl.ds(g * HD, HD)],
                    kv.at[g, part, pl.ds(span * rows, rows), :],
                    own_sem.at[g, part],
                )
            )
    for copy in own:
        copy.start()
    small = [
        pltpu.make_async_copy(source, target, row_sem.at[number])
        for number, (source, target) in enumerate(
            ((seg_hbm, seg_ref), (gain_hbm, gain_ref), (weight_hbm, weight_ref))
        )
    ]
    for copy in small:
        copy.start()
    q_copy.start()

    peers = []
    for db in range(branches):
        for dt in range(tps):
            if db or dt:
                peers.append((lax.rem(b_me + db, branches), lax.rem(t_me + dt, tps)))

    barrier = pltpu.get_barrier_semaphore()

    @pl.when(me >= 2)
    def _():
        pl.semaphore_signal(barrier, inc=1, device_id={"ctx": me - 2}, device_id_type=MESH)

    @pl.when(has_next)
    def _():
        pl.semaphore_signal(barrier, inc=1, device_id={"ctx": me + 2}, device_id_type=MESH)

    pl.semaphore_signal(barrier, inc=1, device_id={"ctx": partner}, device_id_type=MESH)
    for b_to, t_to in peers:
        pl.semaphore_signal(
            barrier, inc=1, device_id={"branch": b_to, "tp": t_to}, device_id_type=MESH
        )

    for copy in small:
        copy.wait()
    lane = lax.broadcasted_iota(jnp.int32, (1, HD), 1)
    segs = seg_ref[...]
    total = segs.shape[0] * segs.shape[1]
    far = 2.0**30
    low = jnp.where(lane == 0, 0.0, jnp.where(lane == 4, -far, far))
    high = jnp.where(lane == 3, float(total), jnp.where(lane == 4, 0.0, -far))
    for rollout in range(1, 4):
        count = jnp.sum((segs < rollout).astype(jnp.float32), axis=1, keepdims=True)
        count = jnp.sum(count, axis=0, keepdims=True)
        low = jnp.where(lane == rollout, count, low)
        high = jnp.where(lane == rollout - 1, count, high)
    place = lax.broadcasted_iota(jnp.int32, (window, HD), 0) + (me - span) * rows
    place = place.astype(jnp.float32)
    member = jnp.where((place >= low) & (place < high), 1.0, 0.0)
    gmask[...] = member.astype(jnp.bfloat16)
    fmask[...] = ((member[span * rows :] - 1.0) * BIG).astype(jnp.bfloat16)
    squares[...] = jnp.zeros_like(squares)
    scored[...] = jnp.zeros_like(scored)
    vt[:, HD:, :] = jnp.ones((groups, vt.shape[1] - HD, window), jnp.bfloat16)

    for distance in range(1, span + 1):

        @pl.when(me < distance)
        def _(distance=distance):
            kv[:, :, pl.ds((span - distance) * rows, rows), :] = jnp.zeros(
                (groups, 2, rows, HD), jnp.bfloat16
            )

    def col_copy(step, g):
        return pltpu.make_async_remote_copy(
            src_ref=kv.at[g, :, pl.ds((span - 2 * (step - 1)) * rows, rows), :],
            dst_ref=kv.at[g, :, pl.ds((span - 2 * step) * rows, rows), :],
            send_sem=col_send.at[step - 1, g],
            recv_sem=col_recv.at[step - 1, g],
            device_id={"ctx": me + 2},
            device_id_type=MESH,
        )

    def x_copy(u, g):
        first = pl.multiple_of((span - 2 * u - 2 * side) * rows, rows)
        return pltpu.make_async_remote_copy(
            src_ref=kv.at[g, :, pl.ds(first, rows), :],
            dst_ref=kv.at[g, :, pl.ds((span - 2 * u - 1) * rows, rows), :],
            send_sem=x_send.at[u, g],
            recv_sem=x_recv.at[u, g],
            device_id={"ctx": partner},
            device_id_type=MESH,
        )

    pl.semaphore_wait(
        barrier,
        1 + len(peers) + (me >= 2).astype(jnp.int32) + has_next.astype(jnp.int32),
    )

    for g in range(groups):
        own[2 * g].wait()
        own[2 * g + 1].wait()

        @pl.when(has_next)
        def _(g=g):
            col_copy(1, g).start()

        @pl.when(side == 0)
        def _(g=g):
            x_copy(0, g).start()

    def arrive(step, g):
        @pl.when(me >= 2 * step)
        def _():
            col_copy(step, g).wait_recv()
            if step < steps:

                @pl.when(has_next)
                def _():
                    col_copy(step + 1, g).start()

                @pl.when(side == 0)
                def _():
                    x_copy(step, g).start()

            @pl.when(side == 1)
            def _():
                x_copy(step - 1, g).start()

    tri_key = lax.broadcasted_iota(jnp.int32, (half, 2 * half), 0)
    tri_row = lax.broadcasted_iota(jnp.int32, (half, 2 * half), 1)
    causal = tri_key <= lax.rem(tri_row, half)

    def span_of(step, r):
        first, last = (span - 2 * step) * rows, (span - 2 * step + 2) * rows
        if step == 1:
            last = span * rows + (r + 1) * half
        if step == steps:
            first += r * half
        return first, last

    def columns_of(g, index):
        top = g * per_group + 2 * index
        return [pl.ds(pl.multiple_of((top + e) * HD, HD), HD) for e in range(2)]

    def score(step, g, index, r):
        first, last = span_of(step, r)
        lines, keys = pl.ds(r * half, half), pl.ds(first, last - first)
        columns = columns_of(g, index)
        marks = fmask[lines, :]
        query = jnp.concatenate(
            [
                jnp.concatenate([q_vm[lines, columns[0]], q_vm[lines, columns[1]]], axis=0),
                jnp.concatenate([marks, marks], axis=0),
            ],
            axis=1,
        )
        key = jnp.concatenate([kv[g, 0, keys, :], gmask[keys, :]], axis=1)
        scores = lax.dot_general(
            key, query, (((1,), (1,)), ((), ())), preferred_element_type=jnp.float32
        )
        if step == 1:
            body = last - first - half
            scores = jnp.concatenate(
                [scores[:body], jnp.where(causal, scores[body:], -BIG)], axis=0
            )
        return scores

    def mix(step, g, index, r, scores):
        first, last = span_of(step, r)
        lines = pl.ds(r * half, half)
        unit = (g * (per_group // 2) + index) * 2 + r
        peak = jnp.max(scores, axis=0, keepdims=True)
        if step > 1:
            before = best[unit, 0:1, :]
            peak = jnp.maximum(before, peak)
        weights = jnp.exp2((scores - peak) * scale).astype(jnp.bfloat16)
        mixed = jnp.dot(
            vt[g, :, pl.ds(first, last - first)], weights, preferred_element_type=jnp.float32
        )
        if step > 1:
            mixed = mixed + acc[unit] * jnp.exp2((before - peak) * scale)
        if step < steps:
            acc[unit] = mixed
            best[unit, 0:1, :] = peak
            return
        attended = mixed[:HD] * (1.0 / mixed[HD : HD + 1])
        attended = attended.astype(jnp.bfloat16).astype(jnp.float32)
        square = jnp.sum(attended * attended, axis=0, keepdims=True)
        squares[0:1, lines] += square[:, :half] + square[:, half:]
        turned = attended.T
        columns = columns_of(g, index)
        for e in range(2):
            out = turned[e * half : (e + 1) * half]
            att_ref[lines, columns[e]] = out.astype(jnp.bfloat16)
            line = gain_ref[:, columns[e]] * weight_ref[:, columns[e]]
            scored[lines, :] += out * line

    pairs = per_group // 2
    arrive(1, 0)
    q_copy.wait()
    for step in range(1, steps + 1):

        def group(g, carry, step=step):
            @pl.when(me >= 2 * step - 1)
            def _():
                x_copy(step - 1, g).wait_recv()

            keys = pl.ds((span - 2 * step) * rows, (2 + (step == 1)) * rows)
            vt[g, pl.ds(0, HD), keys] = kv[g, 1, keys, :].astype(jnp.float32).T.astype(jnp.bfloat16)

            def walk(part, inner):
                chains = [(2 * part + more, r) for more in range(2) for r in range(2)]
                scores = [score(step, g, *chains[0]), score(step, g, *chains[1])]
                for number, chain in enumerate(chains):
                    mix(step, g, *chain, scores[number])
                    if number + 2 < len(chains):
                        scores.append(score(step, g, *chains[number + 2]))

                @pl.when((part == 0) & (g + 1 < groups))
                def _():
                    arrive(step, g + 1)

                if step < steps:

                    @pl.when((part == 0) & (g + 1 == groups))
                    def _():
                        arrive(step + 1, 0)

                return inner

            lax.fori_loop(0, pairs // 2, walk, 0)
            return carry

        lax.fori_loop(0, groups, group, 0)

    slab = jnp.concatenate(
        [
            squares[0:1, :],
            jnp.sum(scored[...].T, axis=0, keepdims=True),
            jnp.zeros((6, rows), jnp.float32),
        ],
        axis=0,
    )
    stats[mine] = slab

    def stat_copy(number):
        b_to, t_to = peers[number]
        return pltpu.make_async_remote_copy(
            src_ref=stats.at[mine],
            dst_ref=stats.at[mine],
            send_sem=st_send.at[number],
            recv_sem=st_recv.at[number],
            device_id={"branch": b_to, "tp": t_to},
            device_id_type=MESH,
        )

    for number in range(len(peers)):
        stat_copy(number).start()

    for g in range(groups):
        for step in range(1, steps + 1):

            @pl.when(has_next & (me >= 2 * (step - 1)))
            def _(step=step, g=g):
                col_copy(step, g).wait_send()

            @pl.when(me >= 2 * (step - 1 + side))
            def _(step=step, g=g):
                x_copy(step - 1, g).wait_send()

    for number in range(len(peers)):
        stat_copy(number).wait()

    def inverse_of(branch):
        square_sum = stats[branch * tps, 0:1, :]
        score = stats[branch * tps, 1:2, :]
        for t in range(1, tps):
            square_sum = square_sum + stats[branch * tps + t, 0:1, :]
            score = score + stats[branch * tps + t, 1:2, :]
        return lax.rsqrt(square_sum / D + EPSILON), score

    joined = jnp.zeros((1, rows), jnp.float32)
    for branch in range(branches):
        inverse, score = inverse_of(branch)
        joined = joined + inverse * score
    joined_ref[...] = joined
    inverse, _ = inverse_of(b_me)
    inv_ref[...] = jnp.broadcast_to(inverse, (HD, rows)).T


def local(sizes, queries, keys, values, segments, norm_gain, head_weight):
    n, branches, tps, span = sizes
    rows, columns = queries.shape[1:]
    groups = keys.shape[2] // HD
    heads = columns // HD
    window = (span + 1) * rows
    steps = span // 2
    devices = branches * tps
    vmem = pl.BlockSpec(memory_space=pltpu.VMEM)
    hbm = pl.BlockSpec(memory_space=pltpu.HBM)
    seg_rows = segments.reshape(-1, HD)
    dma = pltpu.SemaphoreType.DMA
    attended, inverse, joined = pl.pallas_call(
        functools.partial(kernel, sizes),
        out_shape=(
            jax.ShapeDtypeStruct((rows, columns), jnp.bfloat16),
            jax.ShapeDtypeStruct((rows, HD), jnp.float32),
            jax.ShapeDtypeStruct((1, rows), jnp.float32),
        ),
        in_specs=[hbm] * 6,
        out_specs=(vmem, vmem, vmem),
        scratch_shapes=[
            pltpu.VMEM((rows, columns), jnp.bfloat16),
            pltpu.VMEM((groups, 2, window, HD), jnp.bfloat16),
            pltpu.VMEM((groups, HD + 16, window), jnp.bfloat16),
            pltpu.VMEM((window, HD), jnp.bfloat16),
            pltpu.VMEM((rows, HD), jnp.bfloat16),
            pltpu.VMEM((heads, HD + 16, rows), jnp.float32),
            pltpu.VMEM((heads, 8, rows), jnp.float32),
            pltpu.VMEM((8, rows), jnp.float32),
            pltpu.VMEM((rows, HD), jnp.float32),
            pltpu.VMEM((devices, 8, rows), jnp.float32),
            pltpu.VMEM(seg_rows.shape, jnp.int32),
            pltpu.VMEM(norm_gain.shape, jnp.float32),
            pltpu.VMEM(norm_gain.shape, jnp.float32),
            dma,
            dma((groups, 2)),
            dma((3,)),
            dma((steps, groups)),
            dma((steps, groups)),
            dma((steps, groups)),
            dma((steps, groups)),
            dma((devices - 1,)),
            dma((devices - 1,)),
        ],
        compiler_params=pltpu.CompilerParams(
            collective_id=0, has_side_effects=True, vmem_limit_bytes=60 * 2**20
        ),
        cost_estimate=pl.CostEstimate(
            flops=4 * rows * window * columns,
            bytes_accessed=4 * rows * columns,
            transcendentals=heads * rows * window,
        ),
    )(queries, keys, values, seg_rows, norm_gain, head_weight)
    normed = attended.astype(jnp.float32) * inverse[:, :1] * norm_gain
    return normed.astype(jnp.bfloat16)[None], joined.reshape(rows)


def solution(mesh):
    n = mesh.shape["ctx"]
    sizes = (n, mesh.shape["branch"], mesh.shape["tp"], n // 2)
    return jax.shard_map(
        functools.partial(local, sizes),
        mesh=mesh,
        in_specs=(
            P("branch", "ctx", "tp"),
            P("branch", "ctx", "tp"),
            P("branch", "ctx", "tp"),
            P(),
            P("branch", "tp"),
            P("branch", "tp"),
        ),
        out_specs=(P("branch", "ctx", "tp"), P("ctx")),
        check_vma=False,
    )
```

```python
import functools
import math

import jax
import jax.numpy as jnp
from jax import lax
from jax.experimental import pallas as pl
from jax.experimental.pallas import tpu as pltpu
from jax.sharding import PartitionSpec as P

H = 64
KVH = 8
HD = 128
D = 8192

BIG = 2.0**100
EPSILON = 1e-06
MESH = pl.DeviceIdType.MESH


def kernel(
    sizes, q_hbm, k_hbm, v_hbm, seg_hbm, gain_hbm, weight_hbm,
    att_ref, inv_ref, joined_ref,
    q_vm, kv, vt, gmask, fmask, acc, best, squares, scored, stats, seg_ref, gain_ref, weight_ref,
    q_sem, own_sem, row_sem, col_send, col_recv, x_send, x_recv, st_send, st_recv,
):
    n, branches, tps, span = sizes
    steps = span // 2
    rows = q_vm.shape[0]
    half = rows // 2
    groups = kv.shape[0]
    per_group = H // KVH
    window = kv.shape[2]
    scale = math.log2(math.e) / math.sqrt(HD)
    me = lax.axis_index("ctx")
    b_me, t_me = lax.axis_index("branch"), lax.axis_index("tp")
    side = lax.rem(me, 2)
    partner = me + 1 - 2 * side
    has_next = me + 2 < n
    mine = b_me * tps + t_me

    q_copy = pltpu.make_async_copy(q_hbm.at[0], q_vm, q_sem)
    own = []
    for g in range(groups):
        for part, source in enumerate((k_hbm, v_hbm)):
            own.append(
                pltpu.make_async_copy(
                    source.at[0, :, pl.ds(g * HD, HD)],
                    kv.at[g, part, pl.ds(span * rows, rows), :],
                    own_sem.at[g, part],
                )
            )
    for copy in own:
        copy.start()
    small = [
        pltpu.make_async_copy(source, target, row_sem.at[number])
        for number, (source, target) in enumerate(
            ((seg_hbm, seg_ref), (gain_hbm, gain_ref), (weight_hbm, weight_ref))
        )
    ]
    for copy in small:
        copy.start()
    q_copy.start()

    peers = []
    for db in range(branches):
        for dt in range(tps):
            if db or dt:
                peers.append((lax.rem(b_me + db, branches), lax.rem(t_me + dt, tps)))

    barrier = pltpu.get_barrier_semaphore()

    @pl.when(me >= 2)
    def _():
        pl.semaphore_signal(barrier, inc=1, device_id={"ctx": me - 2}, device_id_type=MESH)

    @pl.when(has_next)
    def _():
        pl.semaphore_signal(barrier, inc=1, device_id={"ctx": me + 2}, device_id_type=MESH)

    pl.semaphore_signal(barrier, inc=1, device_id={"ctx": partner}, device_id_type=MESH)
    for b_to, t_to in peers:
        pl.semaphore_signal(
            barrier, inc=1, device_id={"branch": b_to, "tp": t_to}, device_id_type=MESH
        )

    for copy in small:
        copy.wait()
    lane = lax.broadcasted_iota(jnp.int32, (1, HD), 1)
    segs = seg_ref[...]
    total = segs.shape[0] * segs.shape[1]
    far = 2.0**30
    low = jnp.where(lane == 0, 0.0, jnp.where(lane == 4, -far, far))
    high = jnp.where(lane == 3, float(total), jnp.where(lane == 4, 0.0, -far))
    for rollout in range(1, 4):
        count = jnp.sum((segs < rollout).astype(jnp.float32), axis=1, keepdims=True)
        count = jnp.sum(count, axis=0, keepdims=True)
        low = jnp.where(lane == rollout, count, low)
        high = jnp.where(lane == rollout - 1, count, high)
    place = lax.broadcasted_iota(jnp.int32, (window, HD), 0) + (me - span) * rows
    place = place.astype(jnp.float32)
    member = jnp.where((place >= low) & (place < high), 1.0, 0.0)
    gmask[...] = member.astype(jnp.bfloat16)
    fmask[...] = ((member[span * rows :] - 1.0) * BIG).astype(jnp.bfloat16)
    squares[...] = jnp.zeros_like(squares)
    scored[...] = jnp.zeros_like(scored)
    vt[:, HD:, :] = jnp.ones((groups, vt.shape[1] - HD, window), jnp.bfloat16)

    for distance in range(1, span + 1):

        @pl.when(me < distance)
        def _(distance=distance):
            kv[:, :, pl.ds((span - distance) * rows, rows), :] = jnp.zeros(
                (groups, 2, rows, HD), jnp.bfloat16
            )

    def col_copy(step, g):
        return pltpu.make_async_remote_copy(
            src_ref=kv.at[g, :, pl.ds((span - 2 * (step - 1)) * rows, rows), :],
            dst_ref=kv.at[g, :, pl.ds((span - 2 * step) * rows, rows), :],
            send_sem=col_send.at[step - 1, g],
            recv_sem=col_recv.at[step - 1, g],
            device_id={"ctx": me + 2},
            device_id_type=MESH,
        )

    def x_copy(u, g):
        first = pl.multiple_of((span - 2 * u - 2 * side) * rows, rows)
        return pltpu.make_async_remote_copy(
            src_ref=kv.at[g, :, pl.ds(first, rows), :],
            dst_ref=kv.at[g, :, pl.ds((span - 2 * u - 1) * rows, rows), :],
            send_sem=x_send.at[u, g],
            recv_sem=x_recv.at[u, g],
            device_id={"ctx": partner},
            device_id_type=MESH,
        )

    pl.semaphore_wait(
        barrier,
        1 + len(peers) + (me >= 2).astype(jnp.int32) + has_next.astype(jnp.int32),
    )

    for g in range(groups):
        own[2 * g].wait()
        own[2 * g + 1].wait()

        @pl.when(has_next)
        def _(g=g):
            col_copy(1, g).start()

        @pl.when(side == 0)
        def _(g=g):
            x_copy(0, g).start()

    def arrive(step, g):
        @pl.when(me >= 2 * step)
        def _():
            col_copy(step, g).wait_recv()
            if step < steps:

                @pl.when(has_next)
                def _():
                    col_copy(step + 1, g).start()

                @pl.when(side == 0)
                def _():
                    x_copy(step, g).start()

            @pl.when(side == 1)
            def _():
                x_copy(step - 1, g).start()

    tri_key = lax.broadcasted_iota(jnp.int32, (half, 2 * half), 0)
    tri_row = lax.broadcasted_iota(jnp.int32, (half, 2 * half), 1)
    causal = tri_key <= lax.rem(tri_row, half)

    def span_of(step, r):
        first, last = (span - 2 * step) * rows, (span - 2 * step + 2) * rows
        if step == 1:
            last = span * rows + (r + 1) * half
        if step == steps:
            first += r * half
        return first, last

    def columns_of(g, index):
        top = g * per_group + 2 * index
        return [pl.ds(pl.multiple_of((top + e) * HD, HD), HD) for e in range(2)]

    def score(step, g, index, r):
        first, last = span_of(step, r)
        lines, keys = pl.ds(r * half, half), pl.ds(first, last - first)
        columns = columns_of(g, index)
        marks = fmask[lines, :]
        query = jnp.concatenate(
            [
                jnp.concatenate([q_vm[lines, columns[0]], q_vm[lines, columns[1]]], axis=0),
                jnp.concatenate([marks, marks], axis=0),
            ],
            axis=1,
        )
        key = jnp.concatenate([kv[g, 0, keys, :], gmask[keys, :]], axis=1)
        scores = lax.dot_general(
            key, query, (((1,), (1,)), ((), ())), preferred_element_type=jnp.float32
        )
        if step == 1:
            body = last - first - half
            scores = jnp.concatenate(
                [scores[:body], jnp.where(causal, scores[body:], -BIG)], axis=0
            )
        return scores

    def mix(step, g, index, r, scores):
        first, last = span_of(step, r)
        lines = pl.ds(r * half, half)
        unit = (g * (per_group // 2) + index) * 2 + r
        peak = jnp.max(scores, axis=0, keepdims=True)
        if step > 1:
            before = best[unit, 0:1, :]
            peak = jnp.maximum(before, peak)
        weights = jnp.exp2((scores - peak) * scale).astype(jnp.bfloat16)
        mixed = jnp.dot(
            vt[g, :, pl.ds(first, last - first)], weights, preferred_element_type=jnp.float32
        )
        if step > 1:
            mixed = mixed + acc[unit] * jnp.exp2((before - peak) * scale)
        if step < steps:
            acc[unit] = mixed
            best[unit, 0:1, :] = peak
            return
        attended = mixed[:HD] * (1.0 / mixed[HD : HD + 1])
        attended = attended.astype(jnp.bfloat16).astype(jnp.float32)
        square = jnp.sum(attended * attended, axis=0, keepdims=True)
        squares[0:1, lines] += square[:, :half] + square[:, half:]
        turned = attended.T
        columns = columns_of(g, index)
        for e in range(2):
            out = turned[e * half : (e + 1) * half]
            att_ref[lines, columns[e]] = out.astype(jnp.bfloat16)
            line = gain_ref[:, columns[e]] * weight_ref[:, columns[e]]
            scored[lines, :] += out * line

    pairs = per_group // 2
    arrive(1, 0)
    q_copy.wait()
    for step in range(1, steps + 1):

        def group(g, carry, step=step):
            @pl.when(me >= 2 * step - 1)
            def _():
                x_copy(step - 1, g).wait_recv()

            keys = pl.ds((span - 2 * step) * rows, (2 + (step == 1)) * rows)
            vt[g, pl.ds(0, HD), keys] = kv[g, 1, keys, :].astype(jnp.float32).T.astype(jnp.bfloat16)

            def walk(part, inner):
                @pl.when((part == 0) & (g + 1 < groups))
                def _():
                    arrive(step, g + 1)

                if step < steps:

                    @pl.when((part == 0) & (g + 1 == groups))
                    def _():
                        arrive(step + 1, 0)

                chains = [(2 * part + more, r) for more in range(2) for r in range(2)]
                scores = [score(step, g, *chains[0]), score(step, g, *chains[1])]
                for number, chain in enumerate(chains):
                    mix(step, g, *chain, scores[number])
                    if number + 2 < len(chains):
                        scores.append(score(step, g, *chains[number + 2]))

                return inner

            lax.fori_loop(0, pairs // 2, walk, 0)
            return carry

        lax.fori_loop(0, groups, group, 0)

    slab = jnp.concatenate(
        [
            squares[0:1, :],
            jnp.sum(scored[...].T, axis=0, keepdims=True),
            jnp.zeros((6, rows), jnp.float32),
        ],
        axis=0,
    )
    stats[mine] = slab

    def stat_copy(number):
        b_to, t_to = peers[number]
        return pltpu.make_async_remote_copy(
            src_ref=stats.at[mine],
            dst_ref=stats.at[mine],
            send_sem=st_send.at[number],
            recv_sem=st_recv.at[number],
            device_id={"branch": b_to, "tp": t_to},
            device_id_type=MESH,
        )

    for number in range(len(peers)):
        stat_copy(number).start()

    for g in range(groups):
        for step in range(1, steps + 1):

            @pl.when(has_next & (me >= 2 * (step - 1)))
            def _(step=step, g=g):
                col_copy(step, g).wait_send()

            @pl.when(me >= 2 * (step - 1 + side))
            def _(step=step, g=g):
                x_copy(step - 1, g).wait_send()

    for number in range(len(peers)):
        stat_copy(number).wait()

    def inverse_of(branch):
        square_sum = stats[branch * tps, 0:1, :]
        score = stats[branch * tps, 1:2, :]
        for t in range(1, tps):
            square_sum = square_sum + stats[branch * tps + t, 0:1, :]
            score = score + stats[branch * tps + t, 1:2, :]
        return lax.rsqrt(square_sum / D + EPSILON), score

    joined = jnp.zeros((1, rows), jnp.float32)
    for branch in range(branches):
        inverse, score = inverse_of(branch)
        joined = joined + inverse * score
    joined_ref[...] = joined
    inverse, _ = inverse_of(b_me)
    inv_ref[...] = jnp.broadcast_to(inverse, (HD, rows)).T


def local(sizes, queries, keys, values, segments, norm_gain, head_weight):
    n, branches, tps, span = sizes
    rows, columns = queries.shape[1:]
    groups = keys.shape[2] // HD
    heads = columns // HD
    window = (span + 1) * rows
    steps = span // 2
    devices = branches * tps
    vmem = pl.BlockSpec(memory_space=pltpu.VMEM)
    hbm = pl.BlockSpec(memory_space=pltpu.HBM)
    seg_rows = segments.reshape(-1, HD)
    dma = pltpu.SemaphoreType.DMA
    attended, inverse, joined = pl.pallas_call(
        functools.partial(kernel, sizes),
        out_shape=(
            jax.ShapeDtypeStruct((rows, columns), jnp.bfloat16),
            jax.ShapeDtypeStruct((rows, HD), jnp.float32),
            jax.ShapeDtypeStruct((1, rows), jnp.float32),
        ),
        in_specs=[hbm] * 6,
        out_specs=(vmem, vmem, vmem),
        scratch_shapes=[
            pltpu.VMEM((rows, columns), jnp.bfloat16),
            pltpu.VMEM((groups, 2, window, HD), jnp.bfloat16),
            pltpu.VMEM((groups, HD + 16, window), jnp.bfloat16),
            pltpu.VMEM((window, HD), jnp.bfloat16),
            pltpu.VMEM((rows, HD), jnp.bfloat16),
            pltpu.VMEM((heads, HD + 16, rows), jnp.float32),
            pltpu.VMEM((heads, 8, rows), jnp.float32),
            pltpu.VMEM((8, rows), jnp.float32),
            pltpu.VMEM((rows, HD), jnp.float32),
            pltpu.VMEM((devices, 8, rows), jnp.float32),
            pltpu.VMEM(seg_rows.shape, jnp.int32),
            pltpu.VMEM(norm_gain.shape, jnp.float32),
            pltpu.VMEM(norm_gain.shape, jnp.float32),
            dma,
            dma((groups, 2)),
            dma((3,)),
            dma((steps, groups)),
            dma((steps, groups)),
            dma((steps, groups)),
            dma((steps, groups)),
            dma((devices - 1,)),
            dma((devices - 1,)),
        ],
        compiler_params=pltpu.CompilerParams(
            collective_id=0, has_side_effects=True, vmem_limit_bytes=60 * 2**20
        ),
        cost_estimate=pl.CostEstimate(
            flops=4 * rows * window * columns,
            bytes_accessed=4 * rows * columns,
            transcendentals=heads * rows * window,
        ),
    )(queries, keys, values, seg_rows, norm_gain, head_weight)
    normed = attended.astype(jnp.float32) * inverse[:, :1] * norm_gain
    return normed.astype(jnp.bfloat16)[None], joined.reshape(rows)


def solution(mesh):
    n = mesh.shape["ctx"]
    sizes = (n, mesh.shape["branch"], mesh.shape["tp"], n // 2)
    return jax.shard_map(
        functools.partial(local, sizes),
        mesh=mesh,
        in_specs=(
            P("branch", "ctx", "tp"),
            P("branch", "ctx", "tp"),
            P("branch", "ctx", "tp"),
            P(),
            P("branch", "tp"),
            P("branch", "tp"),
        ),
        out_specs=(P("branch", "ctx", "tp"), P("ctx")),
        check_vma=False,
    )
```

```python
import functools
import math

import jax
import jax.numpy as jnp
from jax import lax
from jax.experimental import pallas as pl
from jax.experimental.pallas import tpu as pltpu
from jax.sharding import PartitionSpec as P

H = 64
KVH = 8
HD = 128
D = 8192

BIG = 2.0**100
EPSILON = 1e-06
MESH = pl.DeviceIdType.MESH


def kernel(
    sizes, q_hbm, k_hbm, v_hbm, seg_hbm, gain_hbm, weight_hbm,
    att_out, inv_ref, joined_ref,
    att_ref, q_vm, kv, vt, gmask, fmask, acc, best, squares, scored, stats, seg_ref, gain_ref, weight_ref,
    q_sem, att_sem, own_sem, row_sem, col_send, col_recv, x_send, x_recv, st_send, st_recv,
):
    n, branches, tps, span = sizes
    steps = span // 2
    rows = q_vm.shape[0]
    half = rows // 2
    groups = kv.shape[0]
    per_group = H // KVH
    window = kv.shape[2]
    scale = math.log2(math.e) / math.sqrt(HD)
    me = lax.axis_index("ctx")
    b_me, t_me = lax.axis_index("branch"), lax.axis_index("tp")
    side = lax.rem(me, 2)
    partner = me + 1 - 2 * side
    has_next = me + 2 < n
    mine = b_me * tps + t_me

    q_copy = pltpu.make_async_copy(q_hbm.at[0], q_vm, q_sem)
    own = []
    for g in range(groups):
        for part, source in enumerate((k_hbm, v_hbm)):
            own.append(
                pltpu.make_async_copy(
                    source.at[0, :, pl.ds(g * HD, HD)],
                    kv.at[g, part, pl.ds(span * rows, rows), :],
                    own_sem.at[g, part],
                )
            )
    for copy in own:
        copy.start()
    small = [
        pltpu.make_async_copy(source, target, row_sem.at[number])
        for number, (source, target) in enumerate(
            ((seg_hbm, seg_ref), (gain_hbm, gain_ref), (weight_hbm, weight_ref))
        )
    ]
    for copy in small:
        copy.start()
    q_copy.start()

    peers = []
    for db in range(branches):
        for dt in range(tps):
            if db or dt:
                peers.append((lax.rem(b_me + db, branches), lax.rem(t_me + dt, tps)))

    barrier = pltpu.get_barrier_semaphore()

    @pl.when(me >= 2)
    def _():
        pl.semaphore_signal(barrier, inc=1, device_id={"ctx": me - 2}, device_id_type=MESH)

    @pl.when(has_next)
    def _():
        pl.semaphore_signal(barrier, inc=1, device_id={"ctx": me + 2}, device_id_type=MESH)

    pl.semaphore_signal(barrier, inc=1, device_id={"ctx": partner}, device_id_type=MESH)
    for b_to, t_to in peers:
        pl.semaphore_signal(
            barrier, inc=1, device_id={"branch": b_to, "tp": t_to}, device_id_type=MESH
        )

    for copy in small:
        copy.wait()
    lane = lax.broadcasted_iota(jnp.int32, (1, HD), 1)
    segs = seg_ref[...]
    total = segs.shape[0] * segs.shape[1]
    far = 2.0**30
    low = jnp.where(lane == 0, 0.0, jnp.where(lane == 4, -far, far))
    high = jnp.where(lane == 3, float(total), jnp.where(lane == 4, 0.0, -far))
    for rollout in range(1, 4):
        count = jnp.sum((segs < rollout).astype(jnp.float32), axis=1, keepdims=True)
        count = jnp.sum(count, axis=0, keepdims=True)
        low = jnp.where(lane == rollout, count, low)
        high = jnp.where(lane == rollout - 1, count, high)
    place = lax.broadcasted_iota(jnp.int32, (window, HD), 0) + (me - span) * rows
    place = place.astype(jnp.float32)
    member = jnp.where((place >= low) & (place < high), 1.0, 0.0)
    gmask[...] = member.astype(jnp.bfloat16)
    fmask[...] = ((member[span * rows :] - 1.0) * BIG).astype(jnp.bfloat16)
    squares[...] = jnp.zeros_like(squares)
    scored[...] = jnp.zeros_like(scored)
    vt[:, HD:, :] = jnp.ones((groups, vt.shape[1] - HD, window), jnp.bfloat16)

    for distance in range(1, span + 1):

        @pl.when(me < distance)
        def _(distance=distance):
            kv[:, :, pl.ds((span - distance) * rows, rows), :] = jnp.zeros(
                (groups, 2, rows, HD), jnp.bfloat16
            )

    def col_copy(step, g):
        return pltpu.make_async_remote_copy(
            src_ref=kv.at[g, :, pl.ds((span - 2 * (step - 1)) * rows, rows), :],
            dst_ref=kv.at[g, :, pl.ds((span - 2 * step) * rows, rows), :],
            send_sem=col_send.at[step - 1, g],
            recv_sem=col_recv.at[step - 1, g],
            device_id={"ctx": me + 2},
            device_id_type=MESH,
        )

    def x_copy(u, g):
        first = pl.multiple_of((span - 2 * u - 2 * side) * rows, rows)
        return pltpu.make_async_remote_copy(
            src_ref=kv.at[g, :, pl.ds(first, rows), :],
            dst_ref=kv.at[g, :, pl.ds((span - 2 * u - 1) * rows, rows), :],
            send_sem=x_send.at[u, g],
            recv_sem=x_recv.at[u, g],
            device_id={"ctx": partner},
            device_id_type=MESH,
        )

    pl.semaphore_wait(
        barrier,
        1 + len(peers) + (me >= 2).astype(jnp.int32) + has_next.astype(jnp.int32),
    )

    for g in range(groups):
        own[2 * g].wait()
        own[2 * g + 1].wait()

        @pl.when(has_next)
        def _(g=g):
            col_copy(1, g).start()

        @pl.when(side == 0)
        def _(g=g):
            x_copy(0, g).start()

    def arrive(step, g):
        @pl.when(me >= 2 * step)
        def _():
            col_copy(step, g).wait_recv()
            if step < steps:

                @pl.when(has_next)
                def _():
                    col_copy(step + 1, g).start()

                @pl.when(side == 0)
                def _():
                    x_copy(step, g).start()

            @pl.when(side == 1)
            def _():
                x_copy(step - 1, g).start()

    tri_key = lax.broadcasted_iota(jnp.int32, (half, 2 * half), 0)
    tri_row = lax.broadcasted_iota(jnp.int32, (half, 2 * half), 1)
    causal = tri_key <= lax.rem(tri_row, half)

    def span_of(step, r):
        first, last = (span - 2 * step) * rows, (span - 2 * step + 2) * rows
        if step == 1:
            last = span * rows + (r + 1) * half
        if step == steps:
            first += r * half
        return first, last

    def columns_of(g, index):
        top = g * per_group + 2 * index
        return [pl.ds(pl.multiple_of((top + e) * HD, HD), HD) for e in range(2)]

    def score(step, g, index, r):
        first, last = span_of(step, r)
        lines, keys = pl.ds(r * half, half), pl.ds(first, last - first)
        columns = columns_of(g, index)
        marks = fmask[lines, :]
        query = jnp.concatenate(
            [
                jnp.concatenate([q_vm[lines, columns[0]], q_vm[lines, columns[1]]], axis=0),
                jnp.concatenate([marks, marks], axis=0),
            ],
            axis=1,
        )
        key = jnp.concatenate([kv[g, 0, keys, :], gmask[keys, :]], axis=1)
        scores = lax.dot_general(
            key, query, (((1,), (1,)), ((), ())), preferred_element_type=jnp.float32
        )
        if step == 1:
            body = last - first - half
            scores = jnp.concatenate(
                [scores[:body], jnp.where(causal, scores[body:], -BIG)], axis=0
            )
        return scores

    def mix(step, g, index, r, scores):
        first, last = span_of(step, r)
        lines = pl.ds(r * half, half)
        unit = (g * (per_group // 2) + index) * 2 + r
        peak = jnp.max(scores, axis=0, keepdims=True)
        if step > 1:
            before = best[unit, 0:1, :]
            peak = jnp.maximum(before, peak)
        weights = jnp.exp2((scores - peak) * scale).astype(jnp.bfloat16)
        mixed = jnp.dot(
            vt[g, :, pl.ds(first, last - first)], weights, preferred_element_type=jnp.float32
        )
        if step > 1:
            mixed = mixed + acc[unit] * jnp.exp2((before - peak) * scale)
        if step < steps:
            acc[unit] = mixed
            best[unit, 0:1, :] = peak
            return
        attended = mixed[:HD] * (1.0 / mixed[HD : HD + 1])
        attended = attended.astype(jnp.bfloat16).astype(jnp.float32)
        square = jnp.sum(attended * attended, axis=0, keepdims=True)
        squares[0:1, lines] += square[:, :half] + square[:, half:]
        turned = attended.T
        columns = columns_of(g, index)
        for e in range(2):
            out = turned[e * half : (e + 1) * half]
            att_ref[lines, columns[e]] = out.astype(jnp.bfloat16)
            line = gain_ref[:, columns[e]] * weight_ref[:, columns[e]]
            scored[lines, :] += out * line

    def att_copy(g):
        wide = per_group * HD
        columns = pl.ds(pl.multiple_of(g * wide, wide), wide)
        return pltpu.make_async_copy(att_ref.at[:, columns], att_out.at[:, columns], att_sem.at[g])

    pairs = per_group // 2
    arrive(1, 0)
    q_copy.wait()
    for step in range(1, steps + 1):

        def group(g, carry, step=step):
            @pl.when(me >= 2 * step - 1)
            def _():
                x_copy(step - 1, g).wait_recv()

            keys = pl.ds((span - 2 * step) * rows, (2 + (step == 1)) * rows)
            vt[g, pl.ds(0, HD), keys] = kv[g, 1, keys, :].astype(jnp.float32).T.astype(jnp.bfloat16)

            def walk(part, inner):
                @pl.when((part == 0) & (g + 1 < groups))
                def _():
                    arrive(step, g + 1)

                if step < steps:

                    @pl.when((part == 0) & (g + 1 == groups))
                    def _():
                        arrive(step + 1, 0)

                chains = [(2 * part + more, r) for more in range(2) for r in range(2)]
                scores = [score(step, g, *chains[0]), score(step, g, *chains[1])]
                for number, chain in enumerate(chains):
                    mix(step, g, *chain, scores[number])
                    if number + 2 < len(chains):
                        scores.append(score(step, g, *chains[number + 2]))

                return inner

            lax.fori_loop(0, pairs // 2, walk, 0)
            if step == steps:
                att_copy(g).start()
            return carry

        lax.fori_loop(0, groups, group, 0)

    slab = jnp.concatenate(
        [
            squares[0:1, :],
            jnp.sum(scored[...].T, axis=0, keepdims=True),
            jnp.zeros((6, rows), jnp.float32),
        ],
        axis=0,
    )
    stats[mine] = slab

    def stat_copy(number):
        b_to, t_to = peers[number]
        return pltpu.make_async_remote_copy(
            src_ref=stats.at[mine],
            dst_ref=stats.at[mine],
            send_sem=st_send.at[number],
            recv_sem=st_recv.at[number],
            device_id={"branch": b_to, "tp": t_to},
            device_id_type=MESH,
        )

    for number in range(len(peers)):
        stat_copy(number).start()

    for g in range(groups):
        for step in range(1, steps + 1):

            @pl.when(has_next & (me >= 2 * (step - 1)))
            def _(step=step, g=g):
                col_copy(step, g).wait_send()

            @pl.when(me >= 2 * (step - 1 + side))
            def _(step=step, g=g):
                x_copy(step - 1, g).wait_send()

    for number in range(len(peers)):
        stat_copy(number).wait()

    for g in range(groups):
        att_copy(g).wait()

    def inverse_of(branch):
        square_sum = stats[branch * tps, 0:1, :]
        score = stats[branch * tps, 1:2, :]
        for t in range(1, tps):
            square_sum = square_sum + stats[branch * tps + t, 0:1, :]
            score = score + stats[branch * tps + t, 1:2, :]
        return lax.rsqrt(square_sum / D + EPSILON), score

    joined = jnp.zeros((1, rows), jnp.float32)
    for branch in range(branches):
        inverse, score = inverse_of(branch)
        joined = joined + inverse * score
    joined_ref[...] = joined
    inverse, _ = inverse_of(b_me)
    inv_ref[...] = jnp.broadcast_to(inverse, (HD, rows)).T


def local(sizes, queries, keys, values, segments, norm_gain, head_weight):
    n, branches, tps, span = sizes
    rows, columns = queries.shape[1:]
    groups = keys.shape[2] // HD
    heads = columns // HD
    window = (span + 1) * rows
    steps = span // 2
    devices = branches * tps
    vmem = pl.BlockSpec(memory_space=pltpu.VMEM)
    hbm = pl.BlockSpec(memory_space=pltpu.HBM)
    seg_rows = segments.reshape(-1, HD)
    dma = pltpu.SemaphoreType.DMA
    attended, inverse, joined = pl.pallas_call(
        functools.partial(kernel, sizes),
        out_shape=(
            jax.ShapeDtypeStruct((rows, columns), jnp.bfloat16),
            jax.ShapeDtypeStruct((rows, HD), jnp.float32),
            jax.ShapeDtypeStruct((1, rows), jnp.float32),
        ),
        in_specs=[hbm] * 6,
        out_specs=(hbm, vmem, vmem),
        scratch_shapes=[
            pltpu.VMEM((rows, columns), jnp.bfloat16),
            pltpu.VMEM((rows, columns), jnp.bfloat16),
            pltpu.VMEM((groups, 2, window, HD), jnp.bfloat16),
            pltpu.VMEM((groups, HD + 16, window), jnp.bfloat16),
            pltpu.VMEM((window, HD), jnp.bfloat16),
            pltpu.VMEM((rows, HD), jnp.bfloat16),
            pltpu.VMEM((heads, HD + 16, rows), jnp.float32),
            pltpu.VMEM((heads, 8, rows), jnp.float32),
            pltpu.VMEM((8, rows), jnp.float32),
            pltpu.VMEM((rows, HD), jnp.float32),
            pltpu.VMEM((devices, 8, rows), jnp.float32),
            pltpu.VMEM(seg_rows.shape, jnp.int32),
            pltpu.VMEM(norm_gain.shape, jnp.float32),
            pltpu.VMEM(norm_gain.shape, jnp.float32),
            dma,
            dma((groups,)),
            dma((groups, 2)),
            dma((3,)),
            dma((steps, groups)),
            dma((steps, groups)),
            dma((steps, groups)),
            dma((steps, groups)),
            dma((devices - 1,)),
            dma((devices - 1,)),
        ],
        compiler_params=pltpu.CompilerParams(
            collective_id=0, has_side_effects=True, vmem_limit_bytes=60 * 2**20
        ),
        cost_estimate=pl.CostEstimate(
            flops=4 * rows * window * columns,
            bytes_accessed=4 * rows * columns,
            transcendentals=heads * rows * window,
        ),
    )(queries, keys, values, seg_rows, norm_gain, head_weight)
    normed = attended.astype(jnp.float32) * inverse[:, :1] * norm_gain
    return normed.astype(jnp.bfloat16)[None], joined.reshape(rows)


def solution(mesh):
    n = mesh.shape["ctx"]
    sizes = (n, mesh.shape["branch"], mesh.shape["tp"], n // 2)
    return jax.shard_map(
        functools.partial(local, sizes),
        mesh=mesh,
        in_specs=(
            P("branch", "ctx", "tp"),
            P("branch", "ctx", "tp"),
            P("branch", "ctx", "tp"),
            P(),
            P("branch", "tp"),
            P("branch", "tp"),
        ),
        out_specs=(P("branch", "ctx", "tp"), P("ctx")),
        check_vma=False,
    )
```
